512 devices in a mesh: row: 16 (over x, y_lo), col: 32 (over z, y_hi, core).
Axes of the slice: x: 4, y: 8 (y_hi: 2, y_lo: 4; y = y_hi * 4 + y_lo), z: 8, core: 2. Of those that a mesh axis runs over, the one named last changes fastest.
Arguments:
- pair_repr: bfloat16 [1280, 1280, 128], P('row', 'col'), may hold values from -6 to 6
- norm_gain: float32 [128], replicated, may hold values from 0.25 to 1.75
- a_gate: bfloat16 [128, 128], replicated, may hold values from -0.5 to 0.5
- a_proj: bfloat16 [128, 128], replicated, may hold values from -0.5 to 0.5
- b_gate: bfloat16 [128, 128], replicated, may hold values from -0.5 to 0.5
- b_proj: bfloat16 [128, 128], replicated, may hold values from -0.5 to 0.5
- out_gate: bfloat16 [128, 128], replicated, may hold values from -0.5 to 0.5
- out_proj: bfloat16 [128, 128], replicated, may hold values from -0.5 to 0.5
- out_gain: float32 [128], replicated, may hold values from 0.25 to 1.75
Outputs:
- mirrored: bfloat16 [1280, 1280, 128], P('row', 'col')
The draws below stay inside these ranges and needn't reach their ends.
All inputs are finite; a program needn't handle non-finite values.
Results may differ from the reference program's by a relative error of at most 0.0083.
Values may be sent and summed in bfloat16 or wider, within the bound.
No kernel may reach another device: no remote copies, remote signals or barrier semaphores. Data moves between devices by JAX's collectives and lax.ppermute only.
A program may use at most 64 MiB of HBM per device.

```python
import jax
import jax.numpy as jnp
from jax import lax

C = 128
NTOK = 1280


def block_levels(key, shape, shards, smallest, top_value):
    gain = 1.0
    for position, blocks in shards:
        steps = jax.random.uniform(jax.random.fold_in(jax.random.fold_in(key, 6), position), (blocks,), jnp.float32, smallest / len(shards), top_value / len(shards))
        gain = gain * jnp.repeat(jnp.exp(steps), shape[position] // blocks).reshape((-1,) + (1,) * (len(shape) - 1 - position))
    return gain


def noise(stream_key, dims, deviation, most, cuts=(), kind=jnp.bfloat16):
    values = deviation * jax.random.normal(stream_key, dims, jnp.float32)
    if cuts:
        values = values * block_levels(stream_key, dims, cuts, -0.22, 0.18)
    return jnp.clip(values, -most, most).astype(kind)


def setup_inputs(seed: int = 0) -> dict:
    keys = jax.random.split(jax.random.key(seed), 10)
    return {
        "pair_repr": noise(keys[0], (NTOK, NTOK, C), 1.0, 6.0, ((0, 16), (1, 32))),
        "norm_gain": jnp.clip(1.0 + 0.15 * jax.random.normal(keys[1], (C,), jnp.float32), 0.25, 1.75),
        "a_gate": noise(keys[2], (C, C), C ** -0.5, 0.5),
        "a_proj": noise(keys[3], (C, C), C ** -0.5, 0.5),
        "b_gate": noise(keys[4], (C, C), C ** -0.5, 0.5),
        "b_proj": noise(keys[5], (C, C), C ** -0.5, 0.5),
        "out_gate": noise(keys[6], (C, C), C ** -0.5, 0.5),
        "out_proj": noise(keys[7], (C, C), C ** -0.5, 0.5),
        "out_gain": jnp.clip(1.0 + 0.15 * jax.random.normal(keys[8], (C,), jnp.float32), 0.25, 1.75),
    }


def layer_norm(values, scale_gain):
    mean_val = lax.optimization_barrier(jnp.mean(values, axis=-1, keepdims=True))
    centred = values - mean_val
    var_val = lax.optimization_barrier(jnp.mean(centred * centred, axis=-1, keepdims=True))
    return centred * jax.lax.rsqrt(var_val + 1e-05) * scale_gain

def gated_proj(flattened, weight_gate, weight_proj):
    gate_val = jnp.dot(flattened, weight_gate, preferred_element_type=jnp.float32)
    proj_val = jnp.dot(flattened, weight_proj, preferred_element_type=jnp.float32)
    return (jax.nn.sigmoid(gate_val) * proj_val).astype(jnp.bfloat16)

def reference(pair_repr, norm_gain, a_gate, a_proj, b_gate, b_proj, out_gate, out_proj, out_gain):
    normed = layer_norm(pair_repr.astype(jnp.float32), norm_gain.astype(jnp.float32)).astype(jnp.bfloat16)
    flattened = normed.reshape(-1, C)
    left = gated_proj(flattened, a_gate, a_proj).reshape(NTOK, NTOK, C)
    right = gated_proj(flattened, b_gate, b_proj).reshape(NTOK, NTOK, C)
    tri = jnp.einsum('ikc,jkc->ijc', left.astype(jnp.float32), right.astype(jnp.float32)).astype(jnp.bfloat16)
    tri_normed = layer_norm(tri.astype(jnp.float32), out_gain.astype(jnp.float32)).astype(jnp.bfloat16)
    gate_val = jnp.dot(flattened, out_gate, preferred_element_type=jnp.float32)
    proj_val = jnp.dot(tri_normed.reshape(-1, C), out_proj, preferred_element_type=jnp.float32)
    update = (jax.nn.sigmoid(gate_val) * proj_val).astype(jnp.bfloat16).reshape(NTOK, NTOK, C)
    return jnp.transpose(update, (1, 0, 2))
```

```python
import jax
import jax.numpy as jnp
from jax import lax
from jax.sharding import Mesh, PartitionSpec as P

PLANE = ("yl", "z", "yh", "core")


def layer_norm(values, scale_gain, axis, shape):
    mean_val = jnp.mean(values, axis=axis, keepdims=True)
    centred = values - mean_val
    var_val = jnp.mean(centred * centred, axis=axis, keepdims=True)
    return centred * jax.lax.rsqrt(var_val + 1e-05) * scale_gain.reshape(shape)


def dot_t(weight, flattened):
    return lax.dot_general(
        weight, flattened, (((0,), (1,)), ((), ())), preferred_element_type=jnp.float32
    )


def gated_t(weight_gate, weight_proj, flattened):
    gate_val = dot_t(weight_gate, flattened)
    return (jax.nn.sigmoid(gate_val) * dot_t(weight_proj, flattened)).astype(jnp.bfloat16)


def plane_swap(chunks):
    return lax.all_to_all(chunks, PLANE, split_axis=0, concat_axis=0, tiled=True)


def gather_x(block):
    up = [(i, (i + 1) % 4) for i in range(4)]
    down = [(i, (i - 1) % 4) for i in range(4)]
    before = lax.ppermute(block, "x", up)
    after = lax.ppermute(block, "x", down)
    half = block.shape[0] // 2
    far = jnp.concatenate(
        [lax.ppermute(before[:half], "x", up), lax.ppermute(after[half:], "x", down)], axis=0
    )
    return [block, before, far, after]


def body(pair_repr, norm_gain, a_gate, a_proj, b_gate, b_proj, out_gate, out_proj, out_gain):
    rows, cols, chans = pair_repr.shape
    cells = rows * cols
    normed = layer_norm(pair_repr.astype(jnp.float32), norm_gain, -1, (1, 1, -1)).astype(jnp.bfloat16)
    flattened = normed.reshape(cells, chans)
    left = plane_swap(gated_t(a_gate, a_proj, flattened))
    right = gated_t(b_gate, b_proj, flattened)
    gate = jax.nn.sigmoid(dot_t(out_gate, flattened)).astype(jnp.bfloat16)
    both = plane_swap(jnp.concatenate([right, gate], axis=1))
    right, gate = both[:, :cells], both[:, cells:]

    def unpack(edge):
        edge = edge.reshape(4, 32, rows, cols)
        return jnp.transpose(edge, (0, 2, 1, 3)).reshape(4 * rows, 32 * cols)

    right = unpack(right)
    lefts = gather_x(unpack(left))
    parts = [
        lax.dot_general(right, l, (((1,), (1,)), ((), ())), preferred_element_type=jnp.float32).astype(jnp.bfloat16)
        for l in lefts
    ]
    x = lax.axis_index("x")
    stacked = jnp.stack(parts)
    order = (x - jnp.arange(4)) % 4
    tri = jnp.take(stacked, order, axis=0)
    tri = tri.reshape(4, 4, rows, 4, 2, rows // 2)
    tri = jnp.transpose(tri, (1, 0, 3, 4, 2, 5)).reshape(128, cells)

    gate = gate.reshape(4, 4, 4 * 2 * cells)
    gate = lax.all_to_all(gate, "x", split_axis=1, concat_axis=1, tiled=True)
    gate = gate.reshape(4, 4, 4, 2, 2, rows // 2, cols)
    gate = jnp.transpose(gate, (2, 1, 0, 4, 3, 6, 5)).reshape(128, cells)

    back = plane_swap(jnp.concatenate([tri, gate], axis=1))
    tri, gate = back[:, :cells], back[:, cells:]
    tri_normed = layer_norm(tri.astype(jnp.float32), out_gain, 0, (-1, 1)).astype(jnp.bfloat16)
    proj_val = lax.dot_general(out_proj, tri_normed, (((0,), (0,)), ((), ())), preferred_element_type=jnp.float32)
    update = (gate.astype(jnp.float32) * proj_val).astype(jnp.bfloat16)
    return jnp.transpose(update).reshape(rows, cols, chans)


def solution(mesh):
    fine = Mesh(mesh.devices.reshape(4, 4, 8, 2, 2), ("x", "yl", "z", "yh", "core"))
    tile = P(("x", "yl"), ("z", "yh", "core"), None)
    return jax.shard_map(
        body,
        mesh=fine,
        in_specs=(tile, P(), P(), P(), P(), P(), P(), P(), P()),
        out_specs=tile,
        check_vma=False,
    )
```

```python
import jax
import jax.numpy as jnp
from jax import lax
from jax.experimental import pallas as pl
from jax.experimental.pallas import tpu as pltpu
from jax.sharding import Mesh, PartitionSpec as P

PLANE = ("zh", "yl", "z0", "yh", "core")
F32 = jnp.float32
BF16 = jnp.bfloat16
ROWS, COLS, CHANS = 80, 40, 128
CELLS = ROWS * COLS
HALF = ROWS // 2
VMEM_LIMIT = 48 * 1024 * 1024


def call(kernel, outs, scratch, flops, args):
    moved = sum(a.size * a.dtype.itemsize for a in (*args, *outs))
    return pl.pallas_call(
        kernel,
        out_shape=outs if len(outs) > 1 else outs[0],
        in_specs=[pl.BlockSpec(memory_space=pltpu.SMEM if a.dtype == jnp.int32 else pltpu.VMEM) for a in args],
        out_specs=[pl.BlockSpec(memory_space=pltpu.VMEM)] * len(outs) if len(outs) > 1 else pl.BlockSpec(memory_space=pltpu.VMEM),
        scratch_shapes=scratch,
        compiler_params=pltpu.CompilerParams(vmem_limit_bytes=VMEM_LIMIT),
        cost_estimate=pl.CostEstimate(flops=flops, bytes_accessed=moved, transcendentals=0),
    )(*args)


def shape(dims, dtype=BF16):
    return jax.ShapeDtypeStruct(dims, dtype)


def dot_nt(weight, cells):
    return lax.dot_general(weight, cells, (((1,), (1,)), ((), ())), preferred_element_type=F32)


def left_kernel(z_ref, gain_ref, gate_ref, proj_ref, left_ref, normed_ref, rows_ref):
    gain = gain_ref[...]
    for t in range(10):
        part = pl.ds(t * 320, 320)
        values = z_ref[part, :].astype(F32)
        centred = values - jnp.mean(values, axis=-1, keepdims=True)
        var_val = jnp.mean(centred * centred, axis=-1, keepdims=True)
        rows_ref[part, :] = centred * lax.rsqrt(var_val + 1e-05) * gain
    for k in range(COLS):
        normed_ref[pl.ds(k * ROWS, ROWS), :] = rows_ref[pl.ds(k, ROWS, stride=COLS), :].astype(BF16)
    for t in range(5):
        part = pl.ds(t * 640, 640)
        cells = normed_ref[part, :]
        edge = jax.nn.sigmoid(dot_nt(gate_ref[...], cells)) * dot_nt(proj_ref[...], cells)
        left_ref[:, part] = edge.astype(BF16)


def right_kernel(normed_ref, gate_ref, proj_ref, out_ref, right_ref, opened_ref, rows_ref):
    for t in range(5):
        part = pl.ds(t * 640, 640)
        cells = normed_ref[part, :]
        rows_ref[part, :] = cells.astype(F32)
        edge = jax.nn.sigmoid(dot_nt(gate_ref[...], cells)) * dot_nt(proj_ref[...], cells)
        right_ref[:, part] = edge.astype(BF16)
    for t in range(5):
        pieces = []
        for q in range(t * 5, t * 5 + 5):
            for h in range(2):
                for g in range(q * 8, q * 8 + 8):
                    pieces.append(rows_ref[pl.ds((g // 5) * ROWS + h * HALF + (g % 5) * 8, 8), :])
        cells = jnp.concatenate(pieces, axis=0).astype(BF16)
        opened_ref[:, pl.ds(t * 640, 640)] = jax.nn.sigmoid(dot_nt(out_ref[...], cells)).astype(BF16)


def lay_out(wide_ref, tall_ref, yl):
    for k in range(COLS):
        for zh in range(4):
            tall_ref[pl.ds(k * 32 + zh * 8, 8), 0:ROWS] = wide_ref[pl.ds(zh * 32 + yl * 8, 8), pl.ds(k * ROWS, ROWS)]


def left_unpack_kernel(first_ref, second_ref, out_ref, wide_ref, tall_ref):
    wide_ref[:, 0 : CELLS // 2] = first_ref[...].astype(F32)
    wide_ref[:, CELLS // 2 : CELLS] = second_ref[...].astype(F32)
    for yl in range(4):
        lay_out(wide_ref, tall_ref, yl)
        for t in range(10):
            block = jnp.transpose(tall_ref[pl.ds(t * 128, 128), :])
            out_ref[pl.ds(yl * ROWS, ROWS), pl.ds(t * 128, 128)] = block[:ROWS].astype(BF16)


def right_unpack_kernel(edge_ref, out_ref, wide_ref, tall_ref):
    wide_ref[...] = edge_ref[...].astype(F32)
    tall_ref[...] = jnp.zeros_like(tall_ref)
    for yl in range(4):
        lay_out(wide_ref, tall_ref, yl)
        out_ref[:, pl.ds(yl * 128, 128)] = tall_ref[...].astype(BF16)


def triangle_kernel(slot_ref, l0, l1, l2a, l2b, l3, right_ref, out_ref, prod_ref, wide_ref):
    right = right_ref[...]
    for n, parts in enumerate(((l0,), (l1,), (l2a, l2b), (l3,))):
        base = 0
        for part in parts:
            size = part.shape[0]
            prod = jnp.dot(part[...], right, preferred_element_type=F32)
            for yl in range(4):
                prod_ref[yl, pl.ds(base, size), :] = prod[:, yl * 128 : (yl + 1) * 128]
            base += size
        for yl in range(4):
            for i in range(HALF):
                wide_ref[pl.ds(yl * 8, 8), pl.ds(i * ROWS, ROWS)] = prod_ref[yl, pl.ds(i, 8, stride=HALF), :][:, :ROWS]
        out_ref[pl.ds(pl.multiple_of(slot_ref[n] * 32, 32), 32), :] = wide_ref[...].astype(BF16)


def turn_kernel(gate_ref, out_ref, in_rows, out_rows):
    for t in range(25):
        in_rows[t] = gate_ref[:, pl.ds(t * 128, 128)].astype(F32)
    low = lax.broadcasted_iota(jnp.int32, (4, 128), 1) < 64
    for t in range(25):
        for x in range(4):
            for mid in range(4):
                zero = in_rows[t, pl.ds(x * 32 + mid * 2, 4, stride=8), :]
                one = in_rows[t, pl.ds(x * 32 + mid * 2 + 1, 4, stride=8), :]
                out_rows[t, pl.ds(x * 32 + mid * 8, 4, stride=2), :] = jnp.where(low, zero, pltpu.roll(one, 64, 1))
                out_rows[t, pl.ds(x * 32 + mid * 8 + 1, 4, stride=2), :] = jnp.where(low, pltpu.roll(zero, 64, 1), one)
        out_ref[:, pl.ds(t * 128, 128)] = out_rows[t].astype(BF16)


def output_kernel(tri_ref, gate_ref, gain_ref, proj_ref, out_ref, prod_ref, open_ref):
    for t in range(25):
        lanes = pl.ds(t * 128, 128)
        values = tri_ref[:, lanes].astype(F32)
        centred = values - jnp.mean(values, axis=0, keepdims=True)
        var_val = jnp.mean(centred * centred, axis=0, keepdims=True)
        normed = (centred * lax.rsqrt(var_val + 1e-05) * gain_ref[...]).astype(BF16)
        prod_ref[lanes, :] = lax.dot_general(normed, proj_ref[...], (((0,), (0,)), ((), ())), preferred_element_type=F32)
        turned = jnp.transpose(gate_ref[:, lanes].astype(F32))
        for core in range(2):
            for g in range(t * 8, t * 8 + 8):
                open_ref[pl.ds((core * 40 + g // 5) * HALF + (g % 5) * 8, 8), :] = turned[core * 64 + (g % 8) * 8 : core * 64 + (g % 8) * 8 + 8]
    for j in range(0, ROWS, 2):
        pair = [prod_ref[pl.ds(j + n, HALF, stride=ROWS), :] * open_ref[pl.ds((j + n) * HALF, HALF), :] for n in range(2)]
        out_ref[pl.ds(j * HALF, ROWS), :] = jnp.concatenate(pair, axis=0).astype(BF16)


def plane_swap(chunks):
    return lax.all_to_all(chunks, PLANE, split_axis=0, concat_axis=0, tiled=True)


def gather_x(block):
    up = [(i, (i + 1) % 4) for i in range(4)]
    down = [(i, (i - 1) % 4) for i in range(4)]
    before = lax.ppermute(block, "x", up)
    after = lax.ppermute(block, "x", down)
    half = block.shape[0] // 2
    return block, before, lax.ppermute(before[:half], "x", up), lax.ppermute(after[half:], "x", down), after


def left_edges(pair, gain, gate, proj):
    return call(left_kernel, (shape((CHANS, CELLS)), shape((CELLS, CHANS))), [pltpu.VMEM((CELLS, CHANS), F32)],
                4 * CELLS * CHANS * CHANS, (pair, gain, gate, proj))


def right_edges(normed, gate, proj, out):
    return call(right_kernel, (shape((CHANS, CELLS)), shape((CHANS, CELLS))), [pltpu.VMEM((CELLS, CHANS), F32)],
                6 * CELLS * CHANS * CHANS, (normed, gate, proj, out))


UNPACK = [pltpu.VMEM((128, CELLS), F32), pltpu.VMEM((1280, 128), F32)]


def left_unpack(first, second):
    return call(left_unpack_kernel, (shape((320, 1280)),), UNPACK, 10**7, (first, second))


def right_unpack(edge):
    return call(right_unpack_kernel, (shape((1280, 512)),), UNPACK, 10**7, (edge,))


def triangle(slots, lefts, right):
    return call(triangle_kernel, (shape((128, CELLS)),), [pltpu.VMEM((4, 320, 128), F32), pltpu.VMEM((32, CELLS), F32)],
                2 * 1280 * 1280 * 512, (slots, *lefts, right))


def turn(gate):
    return call(turn_kernel, (shape((128, CELLS)),), [pltpu.VMEM((25, 128, 128), F32)] * 2, 10**7, (gate,))


def output(tri, gate, gain, proj):
    return call(output_kernel, (shape((CELLS, CHANS)),), [pltpu.VMEM((CELLS, CHANS), F32)] * 2,
                2 * CELLS * CHANS * CHANS, (tri, gate, gain, proj))


def body(pair_repr, norm_gain, a_gate, a_proj, b_gate, b_proj, out_gate, out_proj, out_gain):
    pair = pair_repr.reshape(CELLS, CHANS)
    left, normed = left_edges(pair, norm_gain.reshape(1, CHANS), a_gate.T, a_proj.T)
    left = plane_swap(left.reshape(CHANS, 2, CELLS // 2))
    right, opened = right_edges(normed, b_gate.T, b_proj.T, out_gate.T)
    both = plane_swap(jnp.stack([right, opened], axis=1))
    lefts = gather_x(left_unpack(left[:, 0], left[:, 1]))
    gate = lax.all_to_all(both[:, 1].reshape(4, 32, CELLS), "x", split_axis=0, concat_axis=0, tiled=True)
    right = right_unpack(both[:, 0])
    slots = (lax.axis_index("x") - jnp.arange(4, dtype=jnp.int32)) % 4
    tri = triangle(slots.astype(jnp.int32), lefts, right)
    back = plane_swap(jnp.stack([tri, turn(gate.reshape(128, CELLS))], axis=1))
    update = output(back[:, 0], back[:, 1], out_gain.reshape(CHANS, 1), out_proj)
    return update.reshape(ROWS, COLS, CHANS)


def solution(mesh):
    fine = Mesh(mesh.devices.reshape(4, 4, 4, 2, 2, 2), ("x", "yl", "zh", "z0", "yh", "core"))
    tile = P(("x", "yl"), ("zh", "z0", "yh", "core"), None)
    return jax.shard_map(
        body,
        mesh=fine,
        in_specs=(tile, P(), P(), P(), P(), P(), P(), P(), P()),
        out_specs=tile,
        check_vma=False,
    )
```

```python
import jax
import jax.numpy as jnp
from jax import lax
from jax.experimental import pallas as pl
from jax.experimental.pallas import tpu as pltpu
from jax.sharding import Mesh, PartitionSpec as P

PLANE = ("zh", "yl", "z0", "yh", "core")
F32 = jnp.float32
BF16 = jnp.bfloat16
ROWS, COLS, CHANS = 80, 40, 128
CELLS = ROWS * COLS
HALF = ROWS // 2
SPLIT = 13 * 128
VMEM_LIMIT = 20 * 1024 * 1024


def call(kernel, outs, scratch, flops, args):
    moved = sum(a.size * a.dtype.itemsize for a in (*args, *outs))
    return pl.pallas_call(
        kernel,
        out_shape=outs if len(outs) > 1 else outs[0],
        in_specs=[pl.BlockSpec(memory_space=pltpu.SMEM if a.dtype == jnp.int32 else pltpu.VMEM) for a in args],
        out_specs=[pl.BlockSpec(memory_space=pltpu.VMEM)] * len(outs) if len(outs) > 1 else pl.BlockSpec(memory_space=pltpu.VMEM),
        scratch_shapes=scratch,
        compiler_params=pltpu.CompilerParams(vmem_limit_bytes=VMEM_LIMIT),
        cost_estimate=pl.CostEstimate(flops=flops, bytes_accessed=moved, transcendentals=0),
    )(*args)


def shape(dims, dtype=BF16):
    return jax.ShapeDtypeStruct(dims, dtype)


def dot_nt(weight, cells):
    return lax.dot_general(weight, cells, (((0,), (1,)), ((), ())), preferred_element_type=F32)


def left_kernel(z_ref, gain_ref, gate_ref, proj_ref, left_ref, normed_ref, rows_ref):
    gain = gain_ref[...]
    for t in range(10):
        part = pl.ds(t * 320, 320)
        values = z_ref[part, :].astype(F32)
        centred = values - jnp.mean(values, axis=-1, keepdims=True)
        var_val = jnp.mean(centred * centred, axis=-1, keepdims=True)
        rows_ref[part, :] = centred * lax.rsqrt(var_val + 1e-05) * gain
    for k in range(COLS):
        normed_ref[pl.ds(k * ROWS, ROWS), :] = rows_ref[pl.ds(k, ROWS, stride=COLS), :].astype(BF16)
    left_ref[:, 1, CELLS - SPLIT : SPLIT] = jnp.zeros((CHANS, 2 * SPLIT - CELLS), BF16)
    for half, start, size in ((0, 0, 640), (0, 640, 640), (0, 1280, 384), (1, 0, 640), (1, 640, 640), (1, 1280, 256)):
        cells = normed_ref[pl.ds(half * SPLIT + start, size), :]
        edge = jax.nn.sigmoid(dot_nt(gate_ref[...], cells)) * dot_nt(proj_ref[...], cells)
        left_ref[:, half, pl.ds(start, size)] = edge.astype(BF16)


def right_kernel(normed_ref, gate_ref, proj_ref, out_ref, both_ref, rows_ref):
    for t in range(5):
        part = pl.ds(t * 640, 640)
        cells = normed_ref[part, :]
        rows_ref[part, :] = cells.astype(F32)
        edge = jax.nn.sigmoid(dot_nt(gate_ref[...], cells)) * dot_nt(proj_ref[...], cells)
        both_ref[:, 0, part] = edge.astype(BF16)
    for t in range(5):
        pieces = []
        for q in range(t * 5, t * 5 + 5):
            for h in range(2):
                for g in range(q * 8, q * 8 + 8):
                    pieces.append(rows_ref[pl.ds((g // 5) * ROWS + h * HALF + (g % 5) * 8, 8), :])
        cells = jnp.concatenate(pieces, axis=0).astype(BF16)
        both_ref[:, 1, pl.ds(t * 640, 640)] = jax.nn.sigmoid(dot_nt(out_ref[...], cells)).astype(BF16)


def widen(pairs_ref, lane, wide_ref, start):
    def step(c, _):
        rows = pl.ds(pl.multiple_of(c * 8, 8), 8)
        values = pairs_ref[rows].astype(F32)[:, lane, :]
        wide_ref[rows, start : start + values.shape[-1]] = values
        return 0

    lax.fori_loop(0, 16, step, 0)


def lay_out(wide_ref, tall_ref, yl):
    for k in range(COLS):
        for zh in range(4):
            tall_ref[pl.ds(k * 32 + zh * 8, 8), 0:ROWS] = wide_ref[pl.ds(zh * 32 + yl * 8, 8), pl.ds(k * ROWS, ROWS)]


def left_unpack_kernel(pairs_ref, out_ref, wide_ref, tall_ref):
    widen(pairs_ref, 0, wide_ref, 0)
    widen(pairs_ref, 1, wide_ref, SPLIT)
    for yl in range(4):
        lay_out(wide_ref, tall_ref, yl)
        for t in range(10):
            block = jnp.transpose(tall_ref[pl.ds(t * 128, 128), :])
            out_ref[pl.ds(yl * ROWS, ROWS), pl.ds(t * 128, 128)] = block[:ROWS].astype(BF16)


def right_unpack_kernel(pairs_ref, out_ref, wide_ref, tall_ref):
    widen(pairs_ref, 0, wide_ref, 0)
    tall_ref[...] = jnp.zeros_like(tall_ref)
    for yl in range(4):
        lay_out(wide_ref, tall_ref, yl)
        out_ref[:, pl.ds(yl * 128, 128)] = tall_ref[...].astype(BF16)


def triangle_kernel(slot_ref, l0, l1, l2a, l2b, l3, right_ref, out_ref, prod_ref, wide_ref):
    right = right_ref[...]
    for n, parts in enumerate(((l0,), (l1,), (l2a, l2b), (l3,))):
        base = 0
        for part in parts:
            size = part.shape[0]
            prod = jnp.dot(part[...], right, preferred_element_type=F32)
            for yl in range(4):
                prod_ref[yl, pl.ds(base, size), :] = prod[:, yl * 128 : (yl + 1) * 128]
            base += size
        for yl in range(4):
            for i in range(HALF):
                wide_ref[pl.ds(yl * 8, 8), pl.ds(i * ROWS, ROWS)] = prod_ref[yl, pl.ds(i, 8, stride=HALF), :][:, :ROWS]
        out_ref[pl.ds(pl.multiple_of(slot_ref[n] * 32, 32), 32), :] = wide_ref[...].astype(BF16)


def gate_kernel(pairs_ref, out_ref, wide_ref):
    widen(pairs_ref, 1, wide_ref, 0)
    out_ref[...] = wide_ref[...].astype(BF16)


def turn_kernel(tri_ref, gate_ref, out_ref, in_rows, out_rows):
    for t in range(25):
        in_rows[t] = gate_ref[:, pl.ds(t * 128, 128)].astype(F32)
    low = lax.broadcasted_iota(jnp.int32, (4, 128), 1) < 64
    for t in range(25):
        for x in range(4):
            for mid in range(4):
                zero = in_rows[t, pl.ds(x * 32 + mid * 2, 4, stride=8), :]
                one = in_rows[t, pl.ds(x * 32 + mid * 2 + 1, 4, stride=8), :]
                out_rows[t, pl.ds(x * 32 + mid * 8, 4, stride=2), :] = jnp.where(low, zero, pltpu.roll(one, 64, 1))
                out_rows[t, pl.ds(x * 32 + mid * 8 + 1, 4, stride=2), :] = jnp.where(low, pltpu.roll(zero, 64, 1), one)
        out_ref[:, 1, pl.ds(t * 128, 128)] = out_rows[t].astype(BF16)
    for t in range(5):
        lanes = pl.ds(t * 640, 640)
        out_ref[:, 0, lanes] = tri_ref[:, lanes]


def output_kernel(pairs_ref, gain_ref, proj_ref, out_ref, prod_ref, open_ref, tri_ref, gate_ref):
    widen(pairs_ref, 0, tri_ref, 0)
    widen(pairs_ref, 1, gate_ref, 0)
    for t in range(25):
        lanes = pl.ds(t * 128, 128)
        values = tri_ref[:, lanes]
        centred = values - jnp.mean(values, axis=0, keepdims=True)
        var_val = jnp.mean(centred * centred, axis=0, keepdims=True)
        normed = (centred * lax.rsqrt(var_val + 1e-05) * gain_ref[...]).astype(BF16)
        prod_ref[lanes, :] = lax.dot_general(normed, proj_ref[...], (((0,), (0,)), ((), ())), preferred_element_type=F32)
        turned = jnp.transpose(gate_ref[:, lanes])
        for core in range(2):
            for g in range(t * 8, t * 8 + 8):
                open_ref[pl.ds((core * 40 + g // 5) * HALF + (g % 5) * 8, 8), :] = turned[core * 64 + (g % 8) * 8 : core * 64 + (g % 8) * 8 + 8]
    for j in range(0, ROWS, 2):
        pair = [prod_ref[pl.ds(j + n, HALF, stride=ROWS), :] * open_ref[pl.ds((j + n) * HALF, HALF), :] for n in range(2)]
        out_ref[pl.ds(j * HALF, ROWS), :] = jnp.concatenate(pair, axis=0).astype(BF16)


def plane_swap(chunks):
    return lax.all_to_all(chunks, PLANE, split_axis=0, concat_axis=0, tiled=True)


def gather_x(block):
    up = [(i, (i + 1) % 4) for i in range(4)]
    down = [(i, (i - 1) % 4) for i in range(4)]
    before = lax.ppermute(block, "x", up)
    after = lax.ppermute(block, "x", down)
    half = block.shape[0] // 2
    return block, before, lax.ppermute(before[:half], "x", up), lax.ppermute(after[half:], "x", down), after


def left_edges(pair, gain, gate, proj):
    return call(left_kernel, (shape((CHANS, 2, SPLIT)), shape((CELLS, CHANS))), [pltpu.VMEM((CELLS, CHANS), F32)],
                4 * CELLS * CHANS * CHANS, (pair, gain, gate, proj))


def right_edges(normed, gate, proj, out):
    return call(right_kernel, (shape((CHANS, 2, CELLS)),), [pltpu.VMEM((CELLS, CHANS), F32)],
                6 * CELLS * CHANS * CHANS, (normed, gate, proj, out))


WIDE = pltpu.VMEM((128, CELLS), F32)
TALL = pltpu.VMEM((1280, 128), F32)


def left_unpack(pairs):
    return call(left_unpack_kernel, (shape((320, 1280)),), [pltpu.VMEM((128, 2 * SPLIT), F32), TALL], 10**7, (pairs,))


def right_unpack(pairs):
    return call(right_unpack_kernel, (shape((1280, 512)),), [WIDE, TALL], 10**7, (pairs,))


def gate_unpack(pairs):
    return call(gate_kernel, (shape((128, CELLS)),), [WIDE], 10**7, (pairs,))


def triangle(slots, lefts, right):
    return call(triangle_kernel, (shape((128, CELLS)),), [pltpu.VMEM((4, 320, 128), F32), pltpu.VMEM((32, CELLS), F32)],
                2 * 1280 * 1280 * 512, (slots, *lefts, right))


def turn(tri, gate):
    return call(turn_kernel, (shape((128, 2, CELLS)),), [pltpu.VMEM((25, 128, 128), F32)] * 2, 10**7, (tri, gate))


def output(pairs, gain, proj):
    return call(output_kernel, (shape((CELLS, CHANS)),), [pltpu.VMEM((CELLS, CHANS), F32)] * 2 + [WIDE] * 2,
                2 * CELLS * CHANS * CHANS, (pairs, gain, proj))


def body(pair_repr, norm_gain, a_gate, a_proj, b_gate, b_proj, out_gate, out_proj, out_gain):
    pair = pair_repr.reshape(CELLS, CHANS)
    left, normed = left_edges(pair, norm_gain.reshape(1, CHANS), a_gate, a_proj)
    left = plane_swap(left)
    both = plane_swap(right_edges(normed, b_gate, b_proj, out_gate))
    lefts = gather_x(left_unpack(left))
    both, lefts = lax.optimization_barrier((both, lefts))
    gate = lax.all_to_all(gate_unpack(both).reshape(4, 32, CELLS), "x", split_axis=0, concat_axis=0, tiled=True)
    right = right_unpack(both)
    slots = (lax.axis_index("x") - jnp.arange(4, dtype=jnp.int32)) % 4
    tri = triangle(slots.astype(jnp.int32), lefts, right)
    back = plane_swap(turn(tri, gate.reshape(128, CELLS)))
    update = output(back, out_gain.reshape(CHANS, 1), out_proj)
    return update.reshape(ROWS, COLS, CHANS)


def solution(mesh):
    fine = Mesh(mesh.devices.reshape(4, 4, 4, 2, 2, 2), ("x", "yl", "zh", "z0", "yh", "core"))
    tile = P(("x", "yl"), ("zh", "z0", "yh", "core"), None)
    return jax.shard_map(
        body,
        mesh=fine,
        in_specs=(tile, P(), P(), P(), P(), P(), P(), P(), P()),
        out_specs=tile,
        check_vma=False,
    )
```

```python
import jax
import jax.numpy as jnp
from jax import lax
from jax.experimental import pallas as pl
from jax.experimental.pallas import tpu as pltpu
from jax.sharding import Mesh, PartitionSpec as P

PLANE = ("zh", "yl", "z0", "yh", "core")
F32 = jnp.float32
BF16 = jnp.bfloat16
ROWS, COLS, CHANS = 80, 40, 128
CELLS = ROWS * COLS
HALF = ROWS // 2
SPLIT = 13 * 128
VMEM_LIMIT = 20 * 1024 * 1024


def call(kernel, outs, scratch, flops, args):
    moved = sum(a.size * a.dtype.itemsize for a in (*args, *outs))
    return pl.pallas_call(
        kernel,
        out_shape=outs if len(outs) > 1 else outs[0],
        in_specs=[pl.BlockSpec(memory_space=pltpu.SMEM if a.dtype == jnp.int32 else pltpu.VMEM) for a in args],
        out_specs=[pl.BlockSpec(memory_space=pltpu.VMEM)] * len(outs) if len(outs) > 1 else pl.BlockSpec(memory_space=pltpu.VMEM),
        scratch_shapes=scratch,
        compiler_params=pltpu.CompilerParams(vmem_limit_bytes=VMEM_LIMIT),
        cost_estimate=pl.CostEstimate(flops=flops, bytes_accessed=moved, transcendentals=0),
    )(*args)


def shape(dims, dtype=BF16):
    return jax.ShapeDtypeStruct(dims, dtype)


def dot_nt(weight, cells):
    return lax.dot_general(weight, cells, (((0,), (1,)), ((), ())), preferred_element_type=F32)


def edges_kernel(z_ref, gain_ref, a_gate, a_proj, b_gate, b_proj, pairs_ref, normed_ref, rows_ref):
    gain = gain_ref[...]
    for t in range(10):
        part = pl.ds(t * 320, 320)
        values = z_ref[part, :].astype(F32)
        centred = values - jnp.mean(values, axis=-1, keepdims=True)
        var_val = jnp.mean(centred * centred, axis=-1, keepdims=True)
        rows_ref[part, :] = centred * lax.rsqrt(var_val + 1e-05) * gain
    for k in range(COLS):
        normed_ref[pl.ds(k * ROWS, ROWS), :] = rows_ref[pl.ds(k, ROWS, stride=COLS), :].astype(BF16)
    for t in range(5):
        part = pl.ds(t * 640, 640)
        cells = normed_ref[part, :]
        for row, gate_ref, proj_ref in ((0, a_gate, a_proj), (1, b_gate, b_proj)):
            edge = jax.nn.sigmoid(dot_nt(gate_ref[...], cells)) * dot_nt(proj_ref[...], cells)
            pairs_ref[:, row, part] = edge.astype(BF16)


def widen(pairs_ref, places):
    def step(c, _):
        rows = pl.ds(pl.multiple_of(c * 8, 8), 8)
        values = pairs_ref[rows].astype(F32)
        for n, (wide_ref, start) in places.items():
            wide_ref[rows, start : start + values.shape[-1]] = values[:, n, :]
        return 0

    lax.fori_loop(0, 16, step, 0)


def lay_out(wide_ref, tall_ref, yl):
    for k in range(COLS):
        for zh in range(4):
            tall_ref[pl.ds(k * 32 + zh * 8, 8), 0:ROWS] = wide_ref[pl.ds(zh * 32 + yl * 8, 8), pl.ds(k * ROWS, ROWS)]


def left_unpack_kernel(pairs_ref, out_ref, wide_ref, tall_ref):
    widen(pairs_ref, {0: (wide_ref, 0)})
    for yl in range(4):
        lay_out(wide_ref, tall_ref, yl)
        for t in range(10):
            block = jnp.transpose(tall_ref[pl.ds(t * 128, 128), :])
            block = block[:ROWS].astype(BF16)
            for copy in range(4):
                out_ref[copy, pl.ds(yl * ROWS, ROWS), pl.ds(t * 128, 128)] = block


def right_unpack_kernel(pairs_ref, out_ref, wide_ref, tall_ref):
    widen(pairs_ref, {1: (wide_ref, 0)})
    tall_ref[...] = jnp.zeros_like(tall_ref)
    for yl in range(4):
        lay_out(wide_ref, tall_ref, yl)
        out_ref[:, pl.ds(yl * 128, 128)] = tall_ref[...].astype(BF16)


def triangle_kernel(lefts_ref, right_ref, out_ref, prod_ref, wide_ref):
    right = right_ref[...]
    wide_ref[:, CELLS : 2 * SPLIT] = jnp.zeros((32, 2 * SPLIT - CELLS), F32)
    for n in range(4):
        prod = jnp.dot(lefts_ref[n], right, preferred_element_type=F32)
        for yl in range(4):
            prod_ref[yl] = prod[:, yl * 128 : (yl + 1) * 128]
        for yl in range(4):
            for i in range(HALF):
                wide_ref[pl.ds(yl * 8, 8), pl.ds(i * ROWS, ROWS)] = prod_ref[yl, pl.ds(i, 8, stride=HALF), :][:, :ROWS]
        out_ref[n * 32 : n * 32 + 32, 0, :] = wide_ref[:, 0:SPLIT].astype(BF16)
        out_ref[n * 32 : n * 32 + 32, 1, :] = wide_ref[:, SPLIT : 2 * SPLIT].astype(BF16)


def gate_kernel(place_ref, gain_ref, weight_ref, f0, f1, f2, f3, out_ref, open_ref):
    gain = gain_ref[...]
    for e, moved in enumerate((f0, f1, f2, f3)):
        for k in range(2):
            values = moved[k].astype(F32)
            centred = values - jnp.mean(values, axis=-1, keepdims=True)
            var_val = jnp.mean(centred * centred, axis=-1, keepdims=True)
            normed = (centred * lax.rsqrt(var_val + 1e-05) * gain).astype(BF16)
            opened = jax.nn.sigmoid(jnp.dot(normed, weight_ref[...], preferred_element_type=F32))
            base = (place_ref[4] if k == 0 else 1 - place_ref[4]) * 1600 + place_ref[e] * 400
            open_ref[pl.ds(pl.multiple_of(base, 16), 400), :] = opened
    for j in range(0, ROWS, 2):
        pair = [open_ref[pl.ds(((j + n) // COLS) * 1600 + (j + n) % COLS, HALF, stride=COLS), :] for n in range(2)]
        out_ref[pl.ds(j * HALF, ROWS), :] = jnp.concatenate(pair, axis=0).astype(BF16)


def output_kernel(pairs_ref, gate_ref, gain_ref, proj_ref, out_ref, prod_ref, tri_ref):
    widen(pairs_ref, {0: (tri_ref, 0), 1: (tri_ref, SPLIT)})
    for t in range(25):
        lanes = pl.ds(t * 128, 128)
        values = tri_ref[:, lanes]
        centred = values - jnp.mean(values, axis=0, keepdims=True)
        var_val = jnp.mean(centred * centred, axis=0, keepdims=True)
        normed = (centred * lax.rsqrt(var_val + 1e-05) * gain_ref[...]).astype(BF16)
        prod_ref[lanes, :] = lax.dot_general(normed, proj_ref[...], (((0,), (0,)), ((), ())), preferred_element_type=F32)
    for j in range(0, ROWS, 2):
        rows = pl.ds(j * HALF, ROWS)
        pair = jnp.concatenate([prod_ref[pl.ds(j + n, HALF, stride=ROWS), :] for n in range(2)], axis=0)
        out_ref[rows, :] = (pair * gate_ref[rows, :].astype(F32)).astype(BF16)


def plane_swap(chunks):
    return lax.all_to_all(chunks, PLANE, split_axis=0, concat_axis=0, tiled=True)


UP = [(i, (i + 1) % 4) for i in range(4)]
DOWN = [(i, (i - 1) % 4) for i in range(4)]


PAIRS = shape((128, 2, SPLIT))
WIDE = pltpu.VMEM((128, 2 * SPLIT), F32)
FLAT_WIDE = pltpu.VMEM((128, CELLS), F32)
TALL = pltpu.VMEM((1280, 128), F32)
FLAT = pltpu.VMEM((CELLS, CHANS), F32)


def edges(*args):
    return call(edges_kernel, (shape((CHANS, 2, CELLS)),), [pltpu.VMEM((CELLS, CHANS), BF16), FLAT], 8 * CELLS * CHANS * CHANS, args)


def left_unpack(pairs):
    return call(left_unpack_kernel, (shape((4, 320, 1280)),), [FLAT_WIDE, TALL], 10**7, (pairs,))


def right_unpack(pairs):
    return call(right_unpack_kernel, (shape((1280, 512)),), [FLAT_WIDE, TALL], 10**7, (pairs,))


def triangle(lefts, right):
    scratch = [pltpu.VMEM((4, 320, 128), F32), pltpu.VMEM((32, 2 * SPLIT), F32)]
    return call(triangle_kernel, (PAIRS,), scratch, 2 * 1280 * 1280 * 512, (lefts, right))


def output_gate(*args):
    return call(gate_kernel, (shape((CELLS, CHANS)),), [FLAT], 2 * CELLS * CHANS * CHANS, args)


def output(*args):
    return call(output_kernel, (shape((CELLS, CHANS)),), [FLAT, WIDE], 2 * CELLS * CHANS * CHANS, args)


def pick(parts, index):
    return lax.dynamic_index_in_dim(parts, index, 0, keepdims=False)


def swap_core(pair):
    core = lax.axis_index("core")
    other = lax.ppermute(pick(pair, 1 - core), "core", [(0, 1), (1, 0)])
    return jnp.stack([pick(pair, core), other], axis=1)


def spread_x(pieces):
    x = lax.axis_index("x")
    moved = [lax.ppermute(pick(pieces, (x + d) & 3), "x", [(i, (i + d) % 4) for i in range(4)]) for d in (1, 2, 3)]
    return [pick(pieces, x), *moved]


def cross_plane(parts, steps):
    x, zh = lax.axis_index("x"), lax.axis_index("zh")
    moved = []
    for n in steps:
        perm = []
        for yl in range(4):
            for h in range(4):
                for z0 in range(2):
                    for yh in range(2):
                        source = ((yl * 4 + h) * 2 + z0) * 2 + yh
                        target = (((z0 * 2 + yh) * 4 + (h + n) % 4) * 2 + yl // 2) * 2 + yl % 2
                        perm.append((source, target))
        moved.append(lax.ppermute(pick(parts, (x - zh - n) & 3), ("yl", "zh", "z0", "yh"), perm))
    return moved


def land_x(parts):
    x, zh = lax.axis_index("x"), lax.axis_index("zh")
    parts = jnp.stack(parts)
    return [
        part if e == 0 else lax.ppermute(part, "x", [(i, (i + e) % 4) for i in range(4)])
        for e, part in ((e, pick(parts, (zh - x - e) & 3)) for e in range(4))
    ]


def body(pair_repr, norm_gain, a_gate, a_proj, b_gate, b_proj, out_gate, out_proj, out_gain):
    x = lax.axis_index("x")
    gain = norm_gain.reshape(1, CHANS)
    pairs = plane_swap(edges(pair_repr.reshape(CELLS, CHANS), gain, a_gate, a_proj, b_gate, b_proj))
    spread = jnp.stack(spread_x(swap_core(pair_repr.reshape(2, 4, 400, CHANS))))
    pairs, spread = lax.optimization_barrier((pairs, spread))
    near, far = cross_plane(spread, (0, 1)), cross_plane(spread, (2, 3))
    own, right = left_unpack(pairs), right_unpack(pairs)
    lefts = lax.all_to_all(own, "x", split_axis=0, concat_axis=0)
    right, lefts, near, far = lax.optimization_barrier((right, lefts, near, far))
    slots = ((x - jnp.arange(4, dtype=jnp.int32)) & 3).astype(jnp.int32)
    tri = triangle(lefts, right)
    back = plane_swap(tri)
    place = jnp.concatenate([slots, lax.axis_index("core").astype(jnp.int32)[None]])
    gate = output_gate(place, gain, out_gate, *land_x([*near, *far]))
    update = output(back, gate, out_gain.reshape(CHANS, 1), out_proj)
    return update.reshape(ROWS, COLS, CHANS)


def solution(mesh):
    fine = Mesh(mesh.devices.reshape(4, 4, 4, 2, 2, 2), ("x", "yl", "zh", "z0", "yh", "core"))
    tile = P(("x", "yl"), ("zh", "z0", "yh", "core"), None)
    return jax.shard_map(
        body,
        mesh=fine,
        in_specs=(tile, P(), P(), P(), P(), P(), P(), P(), P()),
        out_specs=tile,
        check_vma=False,
    )
```

```python
import jax
import jax.numpy as jnp
from jax import lax
from jax.experimental import pallas as pl
from jax.experimental.pallas import tpu as pltpu
from jax.sharding import Mesh, PartitionSpec as P

PLANE = ("zh", "yl", "z0", "yh", "core")
F32 = jnp.float32
BF16 = jnp.bfloat16
ROWS, COLS, CHANS = 80, 40, 128
CELLS = ROWS * COLS
HALF = ROWS // 2
SPLIT = 13 * 128
VMEM_LIMIT = 20 * 1024 * 1024
VMEM_MOST = 56 * 1024 * 1024


def call(kernel, outs, scratch, flops, args, far=(), limit=VMEM_LIMIT):
    moved = sum(a.size * a.dtype.itemsize for a in (*args, *outs))
    return pl.pallas_call(
        kernel,
        out_shape=outs if len(outs) > 1 else outs[0],
        in_specs=[pl.BlockSpec(memory_space=pl.ANY if n in far else pltpu.SMEM if a.dtype == jnp.int32 else pltpu.VMEM) for n, a in enumerate(args)],
        out_specs=[pl.BlockSpec(memory_space=pltpu.VMEM)] * len(outs) if len(outs) > 1 else pl.BlockSpec(memory_space=pl.ANY if -1 in far else pltpu.VMEM),
        scratch_shapes=scratch,
        compiler_params=pltpu.CompilerParams(vmem_limit_bytes=limit),
        cost_estimate=pl.CostEstimate(flops=flops, bytes_accessed=moved, transcendentals=0),
    )(*args)


def shape(dims, dtype=BF16):
    return jax.ShapeDtypeStruct(dims, dtype)


def dot_nt(weight, cells):
    return lax.dot_general(weight, cells, (((0,), (1,)), ((), ())), preferred_element_type=F32)


def edges_kernel(*refs):
    sources, pairs_ref, landed, normed_ref, rows_ref, sems = refs[:6], refs[6], refs[7:13], refs[13], refs[14], refs[15]
    z_ref, gain_ref, a_gate, a_proj, b_gate, b_proj = landed
    copies = [pltpu.make_async_copy(source, target, sems.at[n]) for n, (source, target) in enumerate(zip(sources[1:], landed[1:]))]
    parts = [
        pltpu.make_async_copy(sources[0].at[pl.ds(t * 640, 640), :], z_ref.at[pl.ds(t * 640, 640), :], sems.at[5 + t])
        for t in range(5)
    ]
    for copy in (*parts, *copies):
        copy.start()
    copies[0].wait()
    gain = gain_ref[...]
    for t in range(10):
        part = pl.ds(t * 320, 320)
        if t % 2 == 0:
            parts[t // 2].wait()
        values = z_ref[part, :].astype(F32)
        centred = values - jnp.mean(values, axis=-1, keepdims=True)
        var_val = jnp.mean(centred * centred, axis=-1, keepdims=True)
        rows_ref[part, :] = centred * lax.rsqrt(var_val + 1e-05) * gain
    for copy in copies[1:]:
        copy.wait()
    for k in range(COLS):
        normed_ref[pl.ds(k * ROWS, ROWS), :] = rows_ref[pl.ds(k, ROWS, stride=COLS), :].astype(BF16)
    for t in range(5):
        part = pl.ds(t * 640, 640)
        cells = normed_ref[part, :]
        for row, gate_ref, proj_ref in ((0, a_gate, a_proj), (1, b_gate, b_proj)):
            edge = jax.nn.sigmoid(dot_nt(gate_ref[...], cells)) * dot_nt(proj_ref[...], cells)
            pairs_ref[:, row, part] = edge.astype(BF16)


def widen(pairs_ref, places):
    def step(c, _):
        rows = pl.ds(pl.multiple_of(c * 8, 8), 8)
        values = pairs_ref[rows].astype(F32)
        for n, (wide_ref, start) in places.items():
            wide_ref[rows, start : start + values.shape[-1]] = values[:, n, :]
        return 0

    lax.fori_loop(0, 16, step, 0)


def lay_out(wide_ref, tall_ref, yl):
    for k in range(COLS):
        for zh in range(4):
            tall_ref[pl.ds(k * 32 + zh * 8, 8), 0:ROWS] = wide_ref[pl.ds(zh * 32 + yl * 8, 8), pl.ds(k * ROWS, ROWS)]


def left_unpack_kernel(pairs_ref, out_ref, wide_ref, tall_ref, own_ref, sems):
    copies = []
    widen(pairs_ref, {0: (wide_ref, 0)})
    for yl in range(4):
        lay_out(wide_ref, tall_ref, yl)
        for t in range(10):
            block = jnp.transpose(tall_ref[pl.ds(t * 128, 128), :])
            own_ref[pl.ds(yl * ROWS, ROWS), pl.ds(t * 128, 128)] = block[:ROWS].astype(BF16)
        rows = pl.ds(yl * ROWS, ROWS)
        for x in range(4):
            copies.append(pltpu.make_async_copy(own_ref.at[rows, :], out_ref.at[x, rows, :], sems.at[yl * 4 + x]))
            copies[-1].start()
    for copy in copies:
        copy.wait()


def right_unpack_kernel(pairs_ref, out_ref, wide_ref, tall_ref):
    widen(pairs_ref, {1: (wide_ref, 0)})
    tall_ref[...] = jnp.zeros_like(tall_ref)
    for yl in range(4):
        lay_out(wide_ref, tall_ref, yl)
        out_ref[:, pl.ds(yl * 128, 128)] = tall_ref[...].astype(BF16)


def triangle_kernel(lefts_hbm, right_ref, out_ref, prod_ref, wide_ref, lefts_ref, sems):
    copies = [pltpu.make_async_copy(lefts_hbm.at[n], lefts_ref.at[n], sems.at[n]) for n in range(4)]
    for copy in copies:
        copy.start()
    right = right_ref[...]
    wide_ref[:, CELLS : 2 * SPLIT] = jnp.zeros((32, 2 * SPLIT - CELLS), F32)
    for n in range(4):
        copies[n].wait()
        prod = jnp.dot(lefts_ref[n], right, preferred_element_type=F32)
        for yl in range(4):
            prod_ref[yl] = prod[:, yl * 128 : (yl + 1) * 128]
        for yl in range(4):
            for i in range(HALF):
                wide_ref[pl.ds(yl * 8, 8), pl.ds(i * ROWS, ROWS)] = prod_ref[yl, pl.ds(i, 8, stride=HALF), :][:, :ROWS]
        out_ref[n * 32 : n * 32 + 32, 0, :] = wide_ref[:, 0:SPLIT].astype(BF16)
        out_ref[n * 32 : n * 32 + 32, 1, :] = wide_ref[:, SPLIT : 2 * SPLIT].astype(BF16)


def gate_kernel(place_ref, gain_ref, weight_ref, f0, f1, f2, f3, out_ref, open_ref):
    gain = gain_ref[...]
    for e, moved in enumerate((f0, f1, f2, f3)):
        for k in range(2):
            values = moved[k].astype(F32)
            centred = values - jnp.mean(values, axis=-1, keepdims=True)
            var_val = jnp.mean(centred * centred, axis=-1, keepdims=True)
            normed = (centred * lax.rsqrt(var_val + 1e-05) * gain).astype(BF16)
            opened = jax.nn.sigmoid(jnp.dot(normed, weight_ref[...], preferred_element_type=F32))
            base = (place_ref[4] if k == 0 else 1 - place_ref[4]) * 1600 + place_ref[e] * 400
            open_ref[pl.ds(pl.multiple_of(base, 16), 400), :] = opened
    for j in range(0, ROWS, 2):
        pair = [open_ref[pl.ds(((j + n) // COLS) * 1600 + (j + n) % COLS, HALF, stride=COLS), :] for n in range(2)]
        out_ref[pl.ds(j * HALF, ROWS), :] = jnp.concatenate(pair, axis=0).astype(BF16)


def output_kernel(pairs_ref, gate_ref, gain_ref, proj_ref, out_ref, prod_ref, tri_ref):
    widen(pairs_ref, {0: (tri_ref, 0), 1: (tri_ref, SPLIT)})
    for t in range(25):
        lanes = pl.ds(t * 128, 128)
        values = tri_ref[:, lanes]
        centred = values - jnp.mean(values, axis=0, keepdims=True)
        var_val = jnp.mean(centred * centred, axis=0, keepdims=True)
        normed = (centred * lax.rsqrt(var_val + 1e-05) * gain_ref[...]).astype(BF16)
        prod_ref[lanes, :] = lax.dot_general(normed, proj_ref[...], (((0,), (0,)), ((), ())), preferred_element_type=F32)
    for j in range(0, ROWS, 2):
        rows = pl.ds(j * HALF, ROWS)
        pair = jnp.concatenate([prod_ref[pl.ds(j + n, HALF, stride=ROWS), :] for n in range(2)], axis=0)
        out_ref[rows, :] = (pair * gate_ref[rows, :].astype(F32)).astype(BF16)


def plane_swap(chunks):
    return lax.all_to_all(chunks, PLANE, split_axis=0, concat_axis=0, tiled=True)


UP = [(i, (i + 1) % 4) for i in range(4)]
DOWN = [(i, (i - 1) % 4) for i in range(4)]


PAIRS = shape((128, 2, SPLIT))
WIDE = pltpu.VMEM((128, 2 * SPLIT), F32)
FLAT_WIDE = pltpu.VMEM((128, CELLS), F32)
TALL = pltpu.VMEM((1280, 128), F32)
FLAT = pltpu.VMEM((CELLS, CHANS), F32)


def edges(*args):
    landing = [pltpu.VMEM(a.shape, a.dtype) for a in args]
    scratch = [*landing, pltpu.VMEM((CELLS, CHANS), BF16), FLAT, pltpu.SemaphoreType.DMA((10,))]
    return call(edges_kernel, (shape((CHANS, 2, CELLS)),), scratch, 8 * CELLS * CHANS * CHANS, args, range(6), VMEM_MOST)


def left_unpack(pairs):
    return call(left_unpack_kernel, (shape((4, 320, 1280)),), [FLAT_WIDE, TALL, pltpu.VMEM((320, 1280), BF16), pltpu.SemaphoreType.DMA((16,))], 10**7, (pairs,), (-1,), VMEM_MOST)


def right_unpack(pairs):
    return call(right_unpack_kernel, (shape((1280, 512)),), [FLAT_WIDE, TALL], 10**7, (pairs,))


def triangle(lefts, right):
    scratch = [pltpu.VMEM((4, 320, 128), F32), pltpu.VMEM((32, 2 * SPLIT), F32), pltpu.VMEM((4, 320, 1280), BF16), pltpu.SemaphoreType.DMA((4,))]
    return call(triangle_kernel, (PAIRS,), scratch, 2 * 1280 * 1280 * 512, (lefts, right), (0,))


def output_gate(*args):
    return call(gate_kernel, (shape((CELLS, CHANS)),), [FLAT], 2 * CELLS * CHANS * CHANS, args)


def output(*args):
    return call(output_kernel, (shape((CELLS, CHANS)),), [FLAT, WIDE], 2 * CELLS * CHANS * CHANS, args)


def pick(parts, index):
    return lax.dynamic_index_in_dim(parts, index, 0, keepdims=False)


def swap_core(pair):
    core = lax.axis_index("core")
    other = lax.ppermute(pick(pair, 1 - core), "core", [(0, 1), (1, 0)])
    return jnp.stack([pick(pair, core), other], axis=1)


def spread_x(pieces):
    x = lax.axis_index("x")
    moved = [lax.ppermute(pick(pieces, (x + d) & 3), "x", [(i, (i + d) % 4) for i in range(4)]) for d in (1, 2, 3)]
    return [pick(pieces, x), *moved]


def cross_plane(parts, steps):
    x, zh = lax.axis_index("x"), lax.axis_index("zh")
    moved = []
    for n in steps:
        perm = []
        for yl in range(4):
            for h in range(4):
                for z0 in range(2):
                    for yh in range(2):
                        source = ((yl * 4 + h) * 2 + z0) * 2 + yh
                        target = (((z0 * 2 + yh) * 4 + (h + n) % 4) * 2 + yl // 2) * 2 + yl % 2
                        perm.append((source, target))
        moved.append(lax.ppermute(pick(parts, (x - zh - n) & 3), ("yl", "zh", "z0", "yh"), perm))
    return moved


def land_x(parts):
    x, zh = lax.axis_index("x"), lax.axis_index("zh")
    parts = jnp.stack(parts)
    return [
        part if e == 0 else lax.ppermute(part, "x", [(i, (i + e) % 4) for i in range(4)])
        for e, part in ((e, pick(parts, (zh - x - e) & 3)) for e in range(4))
    ]


def body(pair_repr, norm_gain, a_gate, a_proj, b_gate, b_proj, out_gate, out_proj, out_gain):
    x = lax.axis_index("x")
    gain = norm_gain.reshape(1, CHANS)
    pairs = plane_swap(edges(pair_repr.reshape(CELLS, CHANS), gain, a_gate, a_proj, b_gate, b_proj))
    spread = jnp.stack(spread_x(swap_core(pair_repr.reshape(2, 4, 400, CHANS))))
    pairs, spread = lax.optimization_barrier((pairs, spread))
    near, far = cross_plane(spread, (0, 1)), cross_plane(spread, (2, 3))
    own, right = left_unpack(pairs), right_unpack(pairs)
    lefts = lax.all_to_all(own, "x", split_axis=0, concat_axis=0)
    slots = ((x - jnp.arange(4, dtype=jnp.int32)) & 3).astype(jnp.int32)
    tri = triangle(lefts, right)
    tri, near, far = lax.optimization_barrier((tri, near, far))
    back = plane_swap(tri)
    place = jnp.concatenate([slots, lax.axis_index("core").astype(jnp.int32)[None]])
    gate = output_gate(place, gain, out_gate, *land_x([*near, *far]))
    update = output(back, gate, out_gain.reshape(CHANS, 1), out_proj)
    return update.reshape(ROWS, COLS, CHANS)


def solution(mesh):
    fine = Mesh(mesh.devices.reshape(4, 4, 4, 2, 2, 2), ("x", "yl", "zh", "z0", "yh", "core"))
    tile = P(("x", "yl"), ("zh", "z0", "yh", "core"), None)
    return jax.shard_map(
        body,
        mesh=fine,
        in_specs=(tile, P(), P(), P(), P(), P(), P(), P(), P()),
        out_specs=tile,
        check_vma=False,
    )
```

```python
import jax
import jax.numpy as jnp
from jax import lax
from jax.experimental import pallas as pl
from jax.experimental.pallas import tpu as pltpu
from jax.sharding import Mesh, PartitionSpec as P

PLANE = ("zh", "yl", "z0", "yh", "core")
F32 = jnp.float32
BF16 = jnp.bfloat16
ROWS, COLS, CHANS = 80, 40, 128
CELLS = ROWS * COLS
HALF = ROWS // 2
SPLIT = 13 * 128
VMEM_LIMIT = 20 * 1024 * 1024
VMEM_MOST = 56 * 1024 * 1024
VMEM_UNPACK = 50 * 1024 * 1024
VMEM_TRIANGLE = 52 * 1024 * 1024


def call(kernel, outs, scratch, flops, args, far=(), limit=VMEM_LIMIT):
    moved = sum(a.size * a.dtype.itemsize for a in (*args, *outs))
    return pl.pallas_call(
        kernel,
        out_shape=outs if len(outs) > 1 else outs[0],
        in_specs=[pl.BlockSpec(memory_space=pl.ANY if n in far else pltpu.SMEM if a.dtype == jnp.int32 else pltpu.VMEM) for n, a in enumerate(args)],
        out_specs=[pl.BlockSpec(memory_space=pltpu.VMEM)] * len(outs) if len(outs) > 1 else pl.BlockSpec(memory_space=pl.ANY if -1 in far else pltpu.VMEM),
        scratch_shapes=scratch,
        compiler_params=pltpu.CompilerParams(vmem_limit_bytes=limit),
        cost_estimate=pl.CostEstimate(flops=flops, bytes_accessed=moved, transcendentals=0),
    )(*args)


def shape(dims, dtype=BF16):
    return jax.ShapeDtypeStruct(dims, dtype)


def dot_nt(weight, cells):
    return lax.dot_general(weight, cells, (((0,), (1,)), ((), ())), preferred_element_type=F32)


def edges_kernel(*refs):
    sources, pairs_ref, landed, normed_ref, rows_ref, sems = refs[:6], refs[6], refs[7:13], refs[13], refs[14], refs[15]
    z_ref, gain_ref, a_gate, a_proj, b_gate, b_proj = landed
    copies = [pltpu.make_async_copy(source, target, sems.at[n]) for n, (source, target) in enumerate(zip(sources[1:], landed[1:]))]
    parts = [
        pltpu.make_async_copy(sources[0].at[pl.ds(t * 640, 640), :], z_ref.at[pl.ds(t * 640, 640), :], sems.at[5 + t])
        for t in range(5)
    ]
    for copy in (*parts, *copies):
        copy.start()
    copies[0].wait()
    gain = gain_ref[...]
    for t in range(10):
        part = pl.ds(t * 320, 320)
        if t % 2 == 0:
            parts[t // 2].wait()
        values = z_ref[part, :].astype(F32)
        centred = values - jnp.mean(values, axis=-1, keepdims=True)
        var_val = jnp.mean(centred * centred, axis=-1, keepdims=True)
        rows_ref[part, :] = centred * lax.rsqrt(var_val + 1e-05) * gain
    for copy in copies[1:]:
        copy.wait()
    for k in range(COLS):
        normed_ref[pl.ds(k * ROWS, ROWS), :] = rows_ref[pl.ds(k, ROWS, stride=COLS), :].astype(BF16)
    for t in range(5):
        part = pl.ds(t * 640, 640)
        cells = normed_ref[part, :]
        for row, gate_ref, proj_ref in ((0, a_gate, a_proj), (1, b_gate, b_proj)):
            edge = jax.nn.sigmoid(dot_nt(gate_ref[...], cells)) * dot_nt(proj_ref[...], cells)
            pairs_ref[:, row, part] = edge.astype(BF16)


def widen(pairs_ref, places):
    def step(c, _):
        rows = pl.ds(pl.multiple_of(c * 8, 8), 8)
        values = pairs_ref[rows].astype(F32)
        for n, (wide_ref, start) in places.items():
            wide_ref[rows, start : start + values.shape[-1]] = values[:, n, :]
        return 0

    lax.fori_loop(0, 16, step, 0)


def lay_out(wide_ref, tall_ref, yl):
    for k in range(COLS):
        for zh in range(4):
            tall_ref[pl.ds(k * 32 + zh * 8, 8), 0:ROWS] = wide_ref[pl.ds(zh * 32 + yl * 8, 8), pl.ds(k * ROWS, ROWS)]


def left_unpack_kernel(pairs_ref, out_ref, wide_ref, tall_ref, own_ref, sems):
    copies = []
    widen(pairs_ref, {0: (wide_ref, 0)})
    for yl in range(4):
        lay_out(wide_ref, tall_ref, yl)
        for t in range(10):
            block = jnp.transpose(tall_ref[pl.ds(t * 128, 128), :])
            own_ref[pl.ds(yl * ROWS, ROWS), pl.ds(t * 128, 128)] = block[:ROWS].astype(BF16)
        rows = pl.ds(yl * ROWS, ROWS)
        for x in range(4):
            copies.append(pltpu.make_async_copy(own_ref.at[rows, :], out_ref.at[x, rows, :], sems.at[yl * 4 + x]))
            copies[-1].start()
    for copy in copies:
        copy.wait()


def right_unpack_kernel(pairs_ref, out_ref, wide_ref, tall_ref):
    widen(pairs_ref, {1: (wide_ref, 0)})
    tall_ref[...] = jnp.zeros_like(tall_ref)
    for yl in range(4):
        lay_out(wide_ref, tall_ref, yl)
        out_ref[:, pl.ds(yl * 128, 128)] = tall_ref[...].astype(BF16)


def triangle_kernel(lefts_hbm, right_hbm, out_hbm, prod_ref, wide_ref, lefts_ref, right_ref, out_ref, sems):
    copies = [pltpu.make_async_copy(lefts_hbm.at[n], lefts_ref.at[n], sems.at[n]) for n in range(4)]
    first = pltpu.make_async_copy(right_hbm, right_ref, sems.at[4])
    for copy in (first, *copies):
        copy.start()
    stores = []
    first.wait()
    right = right_ref[...]
    wide_ref[:, CELLS : 2 * SPLIT] = jnp.zeros((32, 2 * SPLIT - CELLS), F32)
    for n in range(4):
        copies[n].wait()
        prod = jnp.dot(lefts_ref[n], right, preferred_element_type=F32)
        for yl in range(4):
            prod_ref[yl] = prod[:, yl * 128 : (yl + 1) * 128]
        for yl in range(4):
            for i in range(HALF):
                wide_ref[pl.ds(yl * 8, 8), pl.ds(i * ROWS, ROWS)] = prod_ref[yl, pl.ds(i, 8, stride=HALF), :][:, :ROWS]
        out_ref[n * 32 : n * 32 + 32, 0, :] = wide_ref[:, 0:SPLIT].astype(BF16)
        out_ref[n * 32 : n * 32 + 32, 1, :] = wide_ref[:, SPLIT : 2 * SPLIT].astype(BF16)
        rows = pl.ds(n * 32, 32)
        stores.append(pltpu.make_async_copy(out_ref.at[rows], out_hbm.at[rows], sems.at[5 + n]))
        stores[-1].start()
    for store in stores:
        store.wait()


def gate_kernel(place_ref, gain_ref, weight_ref, f0, f1, f2, f3, out_ref, open_ref):
    gain = gain_ref[...]
    for e, moved in enumerate((f0, f1, f2, f3)):
        for k in range(2):
            values = moved[k].astype(F32)
            centred = values - jnp.mean(values, axis=-1, keepdims=True)
            var_val = jnp.mean(centred * centred, axis=-1, keepdims=True)
            normed = (centred * lax.rsqrt(var_val + 1e-05) * gain).astype(BF16)
            opened = jax.nn.sigmoid(jnp.dot(normed, weight_ref[...], preferred_element_type=F32))
            base = (place_ref[4] if k == 0 else 1 - place_ref[4]) * 1600 + place_ref[e] * 400
            open_ref[pl.ds(pl.multiple_of(base, 16), 400), :] = opened
    for j in range(0, ROWS, 2):
        pair = [open_ref[pl.ds(((j + n) // COLS) * 1600 + (j + n) % COLS, HALF, stride=COLS), :] for n in range(2)]
        out_ref[pl.ds(j * HALF, ROWS), :] = jnp.concatenate(pair, axis=0).astype(BF16)


def output_kernel(pairs_ref, gate_ref, gain_ref, proj_ref, out_ref, prod_ref, tri_ref):
    widen(pairs_ref, {0: (tri_ref, 0), 1: (tri_ref, SPLIT)})
    for t in range(25):
        lanes = pl.ds(t * 128, 128)
        values = tri_ref[:, lanes]
        centred = values - jnp.mean(values, axis=0, keepdims=True)
        var_val = jnp.mean(centred * centred, axis=0, keepdims=True)
        normed = (centred * lax.rsqrt(var_val + 1e-05) * gain_ref[...]).astype(BF16)
        prod_ref[lanes, :] = lax.dot_general(normed, proj_ref[...], (((0,), (0,)), ((), ())), preferred_element_type=F32)
    for j in range(0, ROWS, 2):
        rows = pl.ds(j * HALF, ROWS)
        pair = jnp.concatenate([prod_ref[pl.ds(j + n, HALF, stride=ROWS), :] for n in range(2)], axis=0)
        out_ref[rows, :] = (pair * gate_ref[rows, :].astype(F32)).astype(BF16)


def plane_swap(chunks):
    return lax.all_to_all(chunks, PLANE, split_axis=0, concat_axis=0, tiled=True)


UP = [(i, (i + 1) % 4) for i in range(4)]
DOWN = [(i, (i - 1) % 4) for i in range(4)]


PAIRS = shape((128, 2, SPLIT))
WIDE = pltpu.VMEM((128, 2 * SPLIT), F32)
FLAT_WIDE = pltpu.VMEM((128, CELLS), F32)
TALL = pltpu.VMEM((1280, 128), F32)
FLAT = pltpu.VMEM((CELLS, CHANS), F32)


def edges(*args):
    landing = [pltpu.VMEM(a.shape, a.dtype) for a in args]
    scratch = [*landing, pltpu.VMEM((CELLS, CHANS), BF16), FLAT, pltpu.SemaphoreType.DMA((10,))]
    return call(edges_kernel, (shape((CHANS, 2, CELLS)),), scratch, 8 * CELLS * CHANS * CHANS, args, range(6), VMEM_MOST)


def left_unpack(pairs):
    return call(left_unpack_kernel, (shape((4, 320, 1280)),), [FLAT_WIDE, TALL, pltpu.VMEM((320, 1280), BF16), pltpu.SemaphoreType.DMA((16,))], 10**7, (pairs,), (-1,), VMEM_UNPACK)


def right_unpack(pairs):
    return call(right_unpack_kernel, (shape((1280, 512)),), [FLAT_WIDE, TALL], 10**7, (pairs,))


def triangle(lefts, right):
    scratch = [pltpu.VMEM((4, 320, 128), F32), pltpu.VMEM((32, 2 * SPLIT), F32), pltpu.VMEM((4, 320, 1280), BF16)]
    scratch += [pltpu.VMEM((1280, 512), BF16), pltpu.VMEM(PAIRS.shape, BF16), pltpu.SemaphoreType.DMA((9,))]
    return call(triangle_kernel, (PAIRS,), scratch, 2 * 1280 * 1280 * 512, (lefts, right), (0, 1, -1), VMEM_TRIANGLE)


def output_gate(*args):
    return call(gate_kernel, (shape((CELLS, CHANS)),), [FLAT], 2 * CELLS * CHANS * CHANS, args)


def output(*args):
    return call(output_kernel, (shape((CELLS, CHANS)),), [FLAT, WIDE], 2 * CELLS * CHANS * CHANS, args)


def pick(parts, index):
    return lax.dynamic_index_in_dim(parts, index, 0, keepdims=False)


def swap_core(pair):
    core = lax.axis_index("core")
    other = lax.ppermute(pick(pair, 1 - core), "core", [(0, 1), (1, 0)])
    return jnp.stack([pick(pair, core), other], axis=1)


def spread_x(pieces):
    x = lax.axis_index("x")
    moved = [lax.ppermute(pick(pieces, (x + d) & 3), "x", [(i, (i + d) % 4) for i in range(4)]) for d in (1, 2, 3)]
    return [pick(pieces, x), *moved]


def cross_plane(parts, steps):
    x, zh = lax.axis_index("x"), lax.axis_index("zh")
    moved = []
    for n in steps:
        perm = []
        for yl in range(4):
            for h in range(4):
                for z0 in range(2):
                    for yh in range(2):
                        source = ((yl * 4 + h) * 2 + z0) * 2 + yh
                        target = (((z0 * 2 + yh) * 4 + (h + n) % 4) * 2 + yl // 2) * 2 + yl % 2
                        perm.append((source, target))
        moved.append(lax.ppermute(pick(parts, (x - zh - n) & 3), ("yl", "zh", "z0", "yh"), perm))
    return moved


def land_x(parts):
    x, zh = lax.axis_index("x"), lax.axis_index("zh")
    parts = jnp.stack(parts)
    return [
        part if e == 0 else lax.ppermute(part, "x", [(i, (i + e) % 4) for i in range(4)])
        for e, part in ((e, pick(parts, (zh - x - e) & 3)) for e in range(4))
    ]


def body(pair_repr, norm_gain, a_gate, a_proj, b_gate, b_proj, out_gate, out_proj, out_gain):
    x = lax.axis_index("x")
    gain = norm_gain.reshape(1, CHANS)
    pairs = plane_swap(edges(pair_repr.reshape(CELLS, CHANS), gain, a_gate, a_proj, b_gate, b_proj))
    spread = jnp.stack(spread_x(swap_core(pair_repr.reshape(2, 4, 400, CHANS))))
    pairs, spread = lax.optimization_barrier((pairs, spread))
    near, far = cross_plane(spread, (0, 1)), cross_plane(spread, (2, 3))
    own, right = left_unpack(pairs), right_unpack(pairs)
    lefts = lax.all_to_all(own, "x", split_axis=0, concat_axis=0)
    slots = ((x - jnp.arange(4, dtype=jnp.int32)) & 3).astype(jnp.int32)
    tri = triangle(lefts, right)
    tri, near, far = lax.optimization_barrier((tri, near, far))
    back = plane_swap(tri)
    place = jnp.concatenate([slots, lax.axis_index("core").astype(jnp.int32)[None]])
    gate = output_gate(place, gain, out_gate, *land_x([*near, *far]))
    update = output(back, gate, out_gain.reshape(CHANS, 1), out_proj)
    return update.reshape(ROWS, COLS, CHANS)


def solution(mesh):
    fine = Mesh(mesh.devices.reshape(4, 4, 4, 2, 2, 2), ("x", "yl", "zh", "z0", "yh", "core"))
    tile = P(("x", "yl"), ("zh", "z0", "yh", "core"), None)
    return jax.shard_map(
        body,
        mesh=fine,
        in_specs=(tile, P(), P(), P(), P(), P(), P(), P(), P()),
        out_specs=tile,
        check_vma=False,
    )
```

```python
import jax
import jax.numpy as jnp
from jax import lax
from jax.experimental import pallas as pl
from jax.experimental.pallas import tpu as pltpu
from jax.sharding import Mesh, PartitionSpec as P

PLANE = ("zh", "yl", "z0", "yh", "core")
F32 = jnp.float32
BF16 = jnp.bfloat16
ROWS, COLS, CHANS = 80, 40, 128
CELLS = ROWS * COLS
HALF = ROWS // 2
SPLIT = 13 * 128
VMEM_LIMIT = 20 * 1024 * 1024
VMEM_MOST = 56 * 1024 * 1024
VMEM_UNPACK = 50 * 1024 * 1024
VMEM_TRIANGLE = 52 * 1024 * 1024


def call(kernel, outs, scratch, flops, args, far=(), limit=VMEM_LIMIT):
    moved = sum(a.size * a.dtype.itemsize for a in (*args, *outs))
    return pl.pallas_call(
        kernel,
        out_shape=outs if len(outs) > 1 else outs[0],
        in_specs=[pl.BlockSpec(memory_space=pl.ANY if n in far else pltpu.SMEM if a.dtype == jnp.int32 else pltpu.VMEM) for n, a in enumerate(args)],
        out_specs=[pl.BlockSpec(memory_space=pltpu.VMEM)] * len(outs) if len(outs) > 1 else pl.BlockSpec(memory_space=pl.ANY if -1 in far else pltpu.VMEM),
        scratch_shapes=scratch,
        compiler_params=pltpu.CompilerParams(vmem_limit_bytes=limit),
        cost_estimate=pl.CostEstimate(flops=flops, bytes_accessed=moved, transcendentals=0),
    )(*args)


def shape(dims, dtype=BF16):
    return jax.ShapeDtypeStruct(dims, dtype)


def dot_nt(weight, cells):
    return lax.dot_general(weight, cells, (((0,), (1,)), ((), ())), preferred_element_type=F32)


def edges_kernel(*refs):
    sources, pairs_hbm, landed = refs[:6], refs[6], refs[7:13]
    normed_ref, rows_ref, pairs_ref, sems = refs[13:]
    z_ref, gain_ref, a_gate, a_proj, b_gate, b_proj = landed
    copies = [pltpu.make_async_copy(source, target, sems.at[n]) for n, (source, target) in enumerate(zip(sources[1:], landed[1:]))]
    parts = [
        pltpu.make_async_copy(sources[0].at[pl.ds(t * 640, 640), :], z_ref.at[pl.ds(t * 640, 640), :], sems.at[5 + t])
        for t in range(5)
    ]
    for copy in (*parts, *copies):
        copy.start()
    copies[0].wait()
    gain = gain_ref[...]
    for t in range(10):
        part = pl.ds(t * 320, 320)
        if t % 2 == 0:
            parts[t // 2].wait()
        values = z_ref[part, :].astype(F32)
        centred = values - jnp.mean(values, axis=-1, keepdims=True)
        var_val = jnp.mean(centred * centred, axis=-1, keepdims=True)
        rows_ref[part, :] = centred * lax.rsqrt(var_val + 1e-05) * gain
    for copy in copies[1:]:
        copy.wait()
    stores = []
    for k in range(COLS):
        normed_ref[pl.ds(k * ROWS, ROWS), :] = rows_ref[pl.ds(k, ROWS, stride=COLS), :].astype(BF16)
    for t in range(5):
        part = pl.ds(t * 640, 640)
        cells = normed_ref[part, :]
        for row, gate_ref, proj_ref in ((0, a_gate, a_proj), (1, b_gate, b_proj)):
            edge = jax.nn.sigmoid(dot_nt(gate_ref[...], cells)) * dot_nt(proj_ref[...], cells)
            pairs_ref[:, row, part] = edge.astype(BF16)
        stores.append(pltpu.make_async_copy(pairs_ref.at[:, :, part], pairs_hbm.at[:, :, part], sems.at[10 + t]))
        stores[-1].start()
    for store in stores:
        store.wait()


def widen(pairs_ref, places):
    def step(c, _):
        rows = pl.ds(pl.multiple_of(c * 8, 8), 8)
        values = pairs_ref[rows].astype(F32)
        for n, (wide_ref, start) in places.items():
            wide_ref[rows, start : start + values.shape[-1]] = values[:, n, :]
        return 0

    lax.fori_loop(0, 16, step, 0)


def lay_out(wide_ref, tall_ref, yl):
    for k in range(COLS):
        for zh in range(4):
            tall_ref[pl.ds(k * 32 + zh * 8, 8), 0:ROWS] = wide_ref[pl.ds(zh * 32 + yl * 8, 8), pl.ds(k * ROWS, ROWS)]


def left_unpack_kernel(pairs_ref, out_ref, wide_ref, tall_ref, own_ref, sems):
    copies = []
    widen(pairs_ref, {0: (wide_ref, 0)})
    for yl in range(4):
        lay_out(wide_ref, tall_ref, yl)
        for t in range(10):
            block = jnp.transpose(tall_ref[pl.ds(t * 128, 128), :])
            own_ref[pl.ds(yl * ROWS, ROWS), pl.ds(t * 128, 128)] = block[:ROWS].astype(BF16)
        rows = pl.ds(yl * ROWS, ROWS)
        for x in range(4):
            copies.append(pltpu.make_async_copy(own_ref.at[rows, :], out_ref.at[x, rows, :], sems.at[yl * 4 + x]))
            copies[-1].start()
    for copy in copies:
        copy.wait()


def right_unpack_kernel(pairs_ref, out_ref, wide_ref, tall_ref):
    widen(pairs_ref, {1: (wide_ref, 0)})
    tall_ref[...] = jnp.zeros_like(tall_ref)
    for yl in range(4):
        lay_out(wide_ref, tall_ref, yl)
        out_ref[:, pl.ds(yl * 128, 128)] = tall_ref[...].astype(BF16)


def triangle_kernel(lefts_hbm, right_hbm, out_hbm, prod_ref, wide_ref, lefts_ref, right_ref, out_ref, sems):
    copies = [pltpu.make_async_copy(lefts_hbm.at[n], lefts_ref.at[n], sems.at[n]) for n in range(4)]
    first = pltpu.make_async_copy(right_hbm, right_ref, sems.at[4])
    for copy in (first, *copies):
        copy.start()
    stores = []
    first.wait()
    right = right_ref[...]
    wide_ref[:, CELLS : 2 * SPLIT] = jnp.zeros((32, 2 * SPLIT - CELLS), F32)
    for n in range(4):
        copies[n].wait()
        prod = jnp.dot(lefts_ref[n], right, preferred_element_type=F32)
        for yl in range(4):
            prod_ref[yl] = prod[:, yl * 128 : (yl + 1) * 128]
        for yl in range(4):
            for i in range(HALF):
                wide_ref[pl.ds(yl * 8, 8), pl.ds(i * ROWS, ROWS)] = prod_ref[yl, pl.ds(i, 8, stride=HALF), :][:, :ROWS]
        out_ref[n * 32 : n * 32 + 32, 0, :] = wide_ref[:, 0:SPLIT].astype(BF16)
        out_ref[n * 32 : n * 32 + 32, 1, :] = wide_ref[:, SPLIT : 2 * SPLIT].astype(BF16)
        rows = pl.ds(n * 32, 32)
        stores.append(pltpu.make_async_copy(out_ref.at[rows], out_hbm.at[rows], sems.at[5 + n]))
        stores[-1].start()
    for store in stores:
        store.wait()


def gate_kernel(place_ref, gain_ref, weight_ref, f0, f1, f2, f3, out_ref, open_ref):
    gain = gain_ref[...]
    for e, moved in enumerate((f0, f1, f2, f3)):
        for k in range(2):
            values = moved[k].astype(F32)
            centred = values - jnp.mean(values, axis=-1, keepdims=True)
            var_val = jnp.mean(centred * centred, axis=-1, keepdims=True)
            normed = (centred * lax.rsqrt(var_val + 1e-05) * gain).astype(BF16)
            opened = jax.nn.sigmoid(jnp.dot(normed, weight_ref[...], preferred_element_type=F32))
            base = (place_ref[4] if k == 0 else 1 - place_ref[4]) * 1600 + place_ref[e] * 400
            open_ref[pl.ds(pl.multiple_of(base, 16), 400), :] = opened
    for j in range(0, ROWS, 2):
        pair = [open_ref[pl.ds(((j + n) // COLS) * 1600 + (j + n) % COLS, HALF, stride=COLS), :] for n in range(2)]
        out_ref[pl.ds(j * HALF, ROWS), :] = jnp.concatenate(pair, axis=0).astype(BF16)


def output_kernel(pairs_ref, gate_ref, gain_ref, proj_ref, out_hbm, prod_ref, tri_ref, out_ref, sems):
    stores = []
    widen(pairs_ref, {0: (tri_ref, 0), 1: (tri_ref, SPLIT)})
    for t in range(25):
        lanes = pl.ds(t * 128, 128)
        values = tri_ref[:, lanes]
        centred = values - jnp.mean(values, axis=0, keepdims=True)
        var_val = jnp.mean(centred * centred, axis=0, keepdims=True)
        normed = (centred * lax.rsqrt(var_val + 1e-05) * gain_ref[...]).astype(BF16)
        prod_ref[lanes, :] = lax.dot_general(normed, proj_ref[...], (((0,), (0,)), ((), ())), preferred_element_type=F32)
    for j in range(0, ROWS, 2):
        rows = pl.ds(j * HALF, ROWS)
        pair = jnp.concatenate([prod_ref[pl.ds(j + n, HALF, stride=ROWS), :] for n in range(2)], axis=0)
        out_ref[rows, :] = (pair * gate_ref[rows, :].astype(F32)).astype(BF16)
        if j % 16 == 14:
            part = pl.ds((j // 16) * 640, 640)
            stores.append(pltpu.make_async_copy(out_ref.at[part, :], out_hbm.at[part, :], sems.at[j // 16]))
            stores[-1].start()
    for store in stores:
        store.wait()


def plane_swap(chunks):
    return lax.all_to_all(chunks, PLANE, split_axis=0, concat_axis=0, tiled=True)


UP = [(i, (i + 1) % 4) for i in range(4)]
DOWN = [(i, (i - 1) % 4) for i in range(4)]


PAIRS = shape((128, 2, SPLIT))
WIDE = pltpu.VMEM((128, 2 * SPLIT), F32)
FLAT_WIDE = pltpu.VMEM((128, CELLS), F32)
TALL = pltpu.VMEM((1280, 128), F32)
FLAT = pltpu.VMEM((CELLS, CHANS), F32)


def edges(*args):
    landing = [pltpu.VMEM(a.shape, a.dtype) for a in args]
    scratch = [*landing, pltpu.VMEM((CELLS, CHANS), BF16), FLAT, pltpu.VMEM((CHANS, 2, CELLS), BF16), pltpu.SemaphoreType.DMA((15,))]
    return call(edges_kernel, (shape((CHANS, 2, CELLS)),), scratch, 8 * CELLS * CHANS * CHANS, args, (*range(6), -1), VMEM_MOST)


def left_unpack(pairs):
    return call(left_unpack_kernel, (shape((4, 320, 1280)),), [FLAT_WIDE, TALL, pltpu.VMEM((320, 1280), BF16), pltpu.SemaphoreType.DMA((16,))], 10**7, (pairs,), (-1,), VMEM_UNPACK)


def right_unpack(pairs):
    return call(right_unpack_kernel, (shape((1280, 512)),), [FLAT_WIDE, TALL], 10**7, (pairs,))


def triangle(lefts, right):
    scratch = [pltpu.VMEM((4, 320, 128), F32), pltpu.VMEM((32, 2 * SPLIT), F32), pltpu.VMEM((4, 320, 1280), BF16)]
    scratch += [pltpu.VMEM((1280, 512), BF16), pltpu.VMEM(PAIRS.shape, BF16), pltpu.SemaphoreType.DMA((9,))]
    return call(triangle_kernel, (PAIRS,), scratch, 2 * 1280 * 1280 * 512, (lefts, right), (0, 1, -1), VMEM_TRIANGLE)


def output_gate(*args):
    return call(gate_kernel, (shape((CELLS, CHANS)),), [FLAT], 2 * CELLS * CHANS * CHANS, args)


def output(*args):
    return call(output_kernel, (shape((CELLS, CHANS)),), [FLAT, WIDE, pltpu.VMEM((CELLS, CHANS), BF16), pltpu.SemaphoreType.DMA((5,))], 2 * CELLS * CHANS * CHANS, args, (-1,))


def pick(parts, index):
    return lax.dynamic_index_in_dim(parts, index, 0, keepdims=False)


def swap_core(pair):
    core = lax.axis_index("core")
    other = lax.ppermute(pick(pair, 1 - core), "core", [(0, 1), (1, 0)])
    return jnp.stack([pick(pair, core), other], axis=1)


def spread_x(pieces):
    x = lax.axis_index("x")
    moved = [lax.ppermute(pick(pieces, (x + d) & 3), "x", [(i, (i + d) % 4) for i in range(4)]) for d in (1, 2, 3)]
    return [pick(pieces, x), *moved]


def cross_plane(parts, steps):
    x, zh = lax.axis_index("x"), lax.axis_index("zh")
    moved = []
    for n in steps:
        perm = []
        for yl in range(4):
            for h in range(4):
                for z0 in range(2):
                    for yh in range(2):
                        source = ((yl * 4 + h) * 2 + z0) * 2 + yh
                        target = (((z0 * 2 + yh) * 4 + (h + n) % 4) * 2 + yl // 2) * 2 + yl % 2
                        perm.append((source, target))
        moved.append(lax.ppermute(pick(parts, (x - zh - n) & 3), ("yl", "zh", "z0", "yh"), perm))
    return moved


def land_x(parts):
    x, zh = lax.axis_index("x"), lax.axis_index("zh")
    parts = jnp.stack(parts)
    return [
        part if e == 0 else lax.ppermute(part, "x", [(i, (i + e) % 4) for i in range(4)])
        for e, part in ((e, pick(parts, (zh - x - e) & 3)) for e in range(4))
    ]


def body(pair_repr, norm_gain, a_gate, a_proj, b_gate, b_proj, out_gate, out_proj, out_gain):
    x = lax.axis_index("x")
    gain = norm_gain.reshape(1, CHANS)
    pairs = plane_swap(edges(pair_repr.reshape(CELLS, CHANS), gain, a_gate, a_proj, b_gate, b_proj))
    spread = jnp.stack(spread_x(swap_core(pair_repr.reshape(2, 4, 400, CHANS))))
    pairs, spread = lax.optimization_barrier((pairs, spread))
    near, far = cross_plane(spread, (0, 1)), cross_plane(spread, (2, 3))
    own, right = left_unpack(pairs), right_unpack(pairs)
    lefts = lax.all_to_all(own, "x", split_axis=0, concat_axis=0)
    slots = ((x - jnp.arange(4, dtype=jnp.int32)) & 3).astype(jnp.int32)
    tri = triangle(lefts, right)
    tri, near, far = lax.optimization_barrier((tri, near, far))
    back = plane_swap(tri)
    place = jnp.concatenate([slots, lax.axis_index("core").astype(jnp.int32)[None]])
    gate = output_gate(place, gain, out_gate, *land_x([*near, *far]))
    update = output(back, gate, out_gain.reshape(CHANS, 1), out_proj)
    return update.reshape(ROWS, COLS, CHANS)


def solution(mesh):
    fine = Mesh(mesh.devices.reshape(4, 4, 4, 2, 2, 2), ("x", "yl", "zh", "z0", "yh", "core"))
    tile = P(("x", "yl"), ("zh", "z0", "yh", "core"), None)
    return jax.shard_map(
        body,
        mesh=fine,
        in_specs=(tile, P(), P(), P(), P(), P(), P(), P(), P()),
        out_specs=tile,
        check_vma=False,
    )
```
